32 devices in a mesh: tgt: 4 (over y, core), src: 8 (over z, x).
Axes of the slice: x: 2, y: 2, z: 4, core: 2. Of those that a mesh axis runs over, the one named last changes fastest.
Arguments:
- trial_vectors: float32 [8, 32, 128], P(None, ('tgt', 'src')), may hold values from -18 to 18
- couplings: float32 [32, 8, 128, 128], P('tgt', 'src'), may hold values from -0.25 to 0.25
- neighbours: int32 [32, 8], P('tgt', 'src'), may hold values from 0 to 31, as said below
- live_slots: int32 [32, 8], P('tgt', 'src'), may hold values from 0 to 1, as said below
- energies: float32 [32, 128], P(('tgt', 'src')), may hold values from 1 to 3
Outputs:
- sigma_vectors: float32 [8, 32, 128], P(None, ('tgt', 'src'))
- residual: float32 [8, 32, 128], P(None, ('tgt', 'src'))
- residual_norms: float32 [8], replicated
The draws below stay inside these ranges and needn't reach their ends.
Inputs may be any that keep to these rules, and one draw needn't show every extreme that they name: `neighbours`: each entry differs from its own chromophore's index by at most 4. `live_slots`: some chromophore has all 8 slots live.
All inputs are finite; a program needn't handle non-finite values.
Results may differ from the reference program's by a relative error of at most 0.000062.
Values sent between devices are 32-bit elements; how exact they have to be, the bound alone decides.
No kernel may reach another device: no remote copies, remote signals or barrier semaphores. Data moves between devices by JAX's collectives and lax.ppermute only.
A program may use at most 64 MiB of HBM per device.

```python
import jax
import jax.numpy as jnp
from jax import lax

S = 128
K = 8
NB = 8
M = 32
REACH = 4
N_TGT = 4


def neighbour_table(key):
    inner_key = jax.random.fold_in(key, 7)
    keys_rows = jax.random.split(inner_key, M)
    orders = jax.vmap(lambda subkey: jax.random.permutation(subkey, 2 * REACH))(keys_rows)[:, :NB]
    offsets = jnp.where(orders < REACH, orders - REACH, orders - REACH + 1).astype(jnp.int32)
    row_index = jnp.arange(M, dtype=jnp.int32)[:, None]
    target = row_index + offsets
    inside = (target >= 0) & (target < M)
    counts = jax.random.randint(jax.random.fold_in(key, 11), (M, 1), NB // 2, NB + 1)
    full_row = jax.random.randint(jax.random.fold_in(key, 13), (), REACH, M - REACH)
    counts = jnp.where(row_index == full_row, NB, counts)
    slot_index = jnp.arange(NB, dtype=jnp.int32)[None, :]
    live = ((slot_index < counts) & inside).astype(jnp.int32)
    chosen = jnp.where(inside, target, row_index).astype(jnp.int32)
    return (chosen, live)


def draw_neighbours(key, part):
    return neighbour_table(key)[0]


def draw_live_slots(key, part):
    return neighbour_table(key)[1]


def draw_trial_vectors(key, part):
    first_key = jax.random.fold_in(key, 21)
    position = jnp.arange(M, dtype=jnp.float32) / M
    rising = (3.0 ** position)[None, :, None]
    values = jax.random.normal(first_key, (K, M, S), jnp.float32) * rising
    return jnp.clip(values, -18.0, 18.0).astype(jnp.float32)


def levels(own_key, shape, cuts, low, top_value):
    def one(dim, parts):
        steps = jax.random.uniform(jax.random.fold_in(jax.random.fold_in(own_key, 6), dim), (parts,), jnp.float32, low / len(cuts), top_value / len(cuts))
        return jnp.repeat(jnp.exp(steps), shape[dim] // parts).reshape((-1,) + (1,) * (len(shape) - dim - 1))

    level = one(*cuts[0])
    for cut in cuts[1:]:
        level = level * one(*cut)
    return level


def centred(own_key, shape, spread, reach, shards=(), kind=jnp.bfloat16):
    loudness = levels(own_key, shape, shards, -0.22, 0.18) if shards else 1.0
    values = jax.random.normal(own_key, shape, jnp.float32) * spread * loudness
    return jnp.minimum(jnp.maximum(values, -reach), reach).astype(kind)


def setup_inputs(seed: int = 0) -> dict:
    splits = jax.random.split(jax.random.key(seed), 6)
    trial_vectors = draw_trial_vectors(jax.random.fold_in(splits[5], 71), 0)
    couplings = centred(splits[1], (M, NB, S, S), (S * NB // 2) ** -0.5, 0.25, ((0, 4), (1, 8)), jnp.float32)
    neighbours = draw_neighbours(jax.random.fold_in(splits[5], 71), 0)
    live_slots = draw_live_slots(jax.random.fold_in(splits[5], 71), 0)
    energies = jnp.clip(1.0 + 2.0 * jax.random.uniform(splits[4], (M, S), jnp.float32) ** levels(splits[4], (M, S), ((0, 32),), -0.2, 0.2), 1.0, 3.0)
    return dict(trial_vectors=trial_vectors, couplings=couplings, neighbours=neighbours, live_slots=live_slots, energies=energies)


def reference(trial_vectors, couplings, neighbours, live_slots, energies):
    vectors, chromos, states = trial_vectors.shape
    slot_weight = live_slots.astype(jnp.float32)

    def one_block(pieces):
        tiles, index_rows, weight_rows = pieces
        fetched = jnp.take(trial_vectors, index_rows.reshape(-1), axis=1)
        fetched = fetched.reshape(vectors, index_rows.shape[0], index_rows.shape[1], states)
        fetched = fetched * weight_rows[None, :, :, None]
        return jnp.einsum('inab,kinb->kia', tiles, fetched, precision=lax.Precision.HIGHEST)
    stacked = lax.map(one_block, (couplings.reshape(N_TGT, -1, NB, states, states), neighbours.reshape(N_TGT, -1, NB), slot_weight.reshape(N_TGT, -1, NB)))
    coupled = jnp.transpose(stacked, (1, 0, 2, 3)).reshape(vectors, chromos, states)
    sigmas = coupled + energies[None] * trial_vectors
    projected = jnp.einsum('kia,lia->kl', trial_vectors, sigmas, precision=lax.Precision.HIGHEST)
    metric = jnp.einsum('kia,lia->kl', trial_vectors, trial_vectors, precision=lax.Precision.HIGHEST)
    factor = jnp.linalg.cholesky(metric)
    mixing = jax.scipy.linalg.cho_solve((factor, True), projected)
    residual = sigmas - jnp.einsum('kia,kl->lia', trial_vectors, mixing, precision=lax.Precision.HIGHEST)
    totals = lax.optimization_barrier(jnp.sum(residual * residual, axis=(1, 2)))
    residual_norms = jnp.sqrt(totals / jnp.diagonal(metric))
    return (sigmas, residual, residual_norms)
```

```python
import functools

import jax
import jax.numpy as jnp
from jax import lax
from jax.experimental import pallas as pl
from jax.experimental.pallas import tpu as pltpu
from jax.sharding import PartitionSpec as P

HIGHEST = lax.Precision.HIGHEST
VMEM = pl.BlockSpec(memory_space=pltpu.VMEM)
SMEM = pl.BlockSpec(memory_space=pltpu.SMEM)
LIMIT = 24 * 2**20


def exchange(x, axis, bit):
    count = lax.axis_size(axis)
    return lax.ppermute(x, axis, [(i, i ^ bit) for i in range(count)])


def bits_of(count):
    return [1 << n for n in range(count.bit_length() - 1)]


def place_of(relative, order):
    place = 0
    for n, bit in enumerate(order):
        place = place + jnp.where((relative & bit) != 0, 1 << n, 0)
    return place


def products(order, table, couplings, neighbours, live, energies, partial, block):
    targets, slots = couplings.shape[0], couplings.shape[1]
    own_src = lax.axis_index("src")
    first = lax.axis_index("tgt") * targets
    own = first + own_src
    for i in range(targets):
        block[i] = table[place_of(own ^ (first + i), order)]
        total = None
        for n in range(slots):
            row = table[place_of(own ^ neighbours[i, n], order)]
            row = row * live[i, n].astype(jnp.float32)
            term = lax.dot_general(
                row,
                couplings[i, n],
                (((1,), (1,)), ((), ())),
                precision=HIGHEST,
                preferred_element_type=jnp.float32,
            )
            total = term if total is None else total + term
        partial[i] = total
    partial[own_src] = partial[own_src] + table[0] * energies[...]


def lanes_of(ref):
    return jnp.concatenate([ref[i] for i in range(ref.shape[0])], axis=1)


def contract(left, right):
    return lax.dot_general(
        left,
        right,
        (((1,), (1,)), ((), ())),
        precision=HIGHEST,
        preferred_element_type=jnp.float32,
    )


def invert(table, out):
    rows, vectors, states = table.shape
    metric = jnp.zeros((vectors, vectors), jnp.float32)
    step = 32
    for r in range(0, rows, step):
        part = jnp.concatenate([table[i] for i in range(r, min(r + step, rows))], axis=1)
        metric = metric + contract(part, part)
    eye = (
        lax.broadcasted_iota(jnp.int32, (vectors, vectors), 0)
        == lax.broadcasted_iota(jnp.int32, (vectors, vectors), 1)
    )
    diagonal = jnp.sum(jnp.where(eye, metric, 0.0), axis=1, keepdims=True)
    sublane = lax.broadcasted_iota(jnp.int32, (vectors, states), 0)
    right = table[0]
    lane = lax.broadcasted_iota(jnp.int32, (vectors, states), 1)
    wide = jnp.concatenate(
        [metric, jnp.where(eye, 1.0, 0.0), jnp.zeros((vectors, states - 2 * vectors), jnp.float32)],
        axis=1,
    )
    for j in range(vectors):
        column = wide[:, j : j + 1]
        inverse = 1.0 / wide[j : j + 1, j : j + 1]
        pivot = wide[j : j + 1, :] * inverse
        pivot_right = right[j : j + 1, :] * inverse
        wide = jnp.where(sublane == j, pivot, wide - column * pivot)
        right = jnp.where(sublane == j, pivot_right, right - column * pivot_right)
    out[0:vectors] = right
    out[vectors : 2 * vectors] = pltpu.roll(wide, states - vectors, 1)
    out[2 * vectors : 3 * vectors] = jnp.broadcast_to(diagonal, (vectors, states))


def grams(mine, theirs, block, sigma_block, sigma_own, gram):
    targets, vectors, states = block.shape
    own_src = lax.axis_index("src")
    sigma_block[...] = mine[...] + theirs[...]
    sigma_own[0] = sigma_block[own_src]
    sigmas = lanes_of(sigma_block)
    both = jnp.concatenate([lanes_of(block), sigmas], axis=0)
    small = contract(sigmas, both)
    gram[...] = jnp.concatenate(
        [small, jnp.zeros((vectors, states - 2 * vectors), jnp.float32)], axis=1
    )


def finish(mine, theirs, solved, sigma_own, residual, norms):
    vectors, states = mine.shape
    gram = mine[...] + theirs[...]
    lane = lax.broadcasted_iota(jnp.int32, (vectors, states), 1)
    sublane = lax.broadcasted_iota(jnp.int32, (vectors, states), 0)
    left = sigma_own[0]
    mixing = jnp.zeros((vectors, states), jnp.float32)
    for j in range(vectors):
        column = gram[:, j : j + 1]
        left = left - column * solved[j : j + 1, :]
        mixing = mixing + column * solved[vectors + j : vectors + j + 1, :]
    residual[0] = left
    terms = jnp.where(lane == sublane + vectors, gram, 0.0) - jnp.where(
        lane < vectors, gram * mixing, 0.0
    )
    totals = jnp.sum(terms, axis=1, keepdims=True)
    column = jnp.sqrt(totals / solved[2 * vectors : 3 * vectors, :])
    norms[...] = jnp.sum(
        jnp.where(lane == sublane, column, 0.0), axis=0, keepdims=True
    )


def shards(trial_vectors, couplings, neighbours, live_slots, energies):
    vectors, _, states = trial_vectors.shape
    targets = couplings.shape[0]
    src_count, tgt_count = lax.axis_size("src"), lax.axis_size("tgt")
    f32 = jnp.float32
    params = pltpu.CompilerParams(vmem_limit_bytes=LIMIT)

    def call(body, out_shape, in_specs, out_specs, flops, moved):
        return pl.pallas_call(
            body,
            out_shape=out_shape,
            in_specs=in_specs,
            out_specs=out_specs,
            compiler_params=params,
            cost_estimate=pl.CostEstimate(
                flops=flops, bytes_accessed=moved, transcendentals=0
            ),
        )

    def shape(*dims):
        return jax.ShapeDtypeStruct(dims, f32)

    table = jnp.transpose(trial_vectors, (1, 0, 2))
    order = []
    for bit in reversed(bits_of(src_count)):
        table = jnp.concatenate([table, exchange(table, "src", bit)], axis=0)
        order.append(bit)
    for bit in reversed(bits_of(tgt_count)):
        table = jnp.concatenate([table, exchange(table, "tgt", bit)], axis=0)
        order.append(bit * src_count)

    partial, block = call(
        functools.partial(products, order),
        (shape(targets, vectors, states),) * 2,
        [VMEM, VMEM, SMEM, SMEM, VMEM],
        [VMEM, VMEM],
        2 * couplings.size * vectors,
        4 * couplings.size,
    )(table, couplings, neighbours, live_slots, energies)
    solved = call(
        invert, shape(3 * vectors, states), [VMEM], VMEM, 10**6, 4 * table.size
    )(table)

    for bit in bits_of(src_count):
        theirs = exchange(partial, "src", bit)
        if 2 * bit < src_count:
            partial = partial + theirs
    _, sigma_own, gram = call(
        grams,
        (shape(targets, vectors, states), shape(1, vectors, states), shape(vectors, states)),
        [VMEM] * 3,
        [VMEM] * 3,
        10**6,
        12 * partial.size,
    )(partial, theirs, block)

    for bit in reversed(bits_of(tgt_count)):
        theirs = exchange(gram, "tgt", bit)
        if bit > 1:
            gram = gram + theirs
    residual, norms = call(
        finish,
        (shape(1, vectors, states), shape(1, states)),
        [VMEM] * 4,
        [VMEM] * 2,
        10**4,
        10**5,
    )(gram, theirs, solved, sigma_own)
    back = lambda x: jnp.transpose(x, (1, 0, 2))
    return (back(sigma_own), back(residual), norms[0, :vectors])


def solution(mesh):
    return jax.shard_map(
        shards,
        mesh=mesh,
        in_specs=(
            P(None, ("tgt", "src"), None),
            P("tgt", "src", None, None),
            P("tgt", "src"),
            P("tgt", "src"),
            P(("tgt", "src"), None),
        ),
        out_specs=(P(None, ("tgt", "src"), None), P(None, ("tgt", "src"), None), P()),
        check_vma=False,
    )
```

```python
import jax
import jax.numpy as jnp
from jax import lax
from jax.experimental import pallas as pl
from jax.experimental.pallas import tpu as pltpu
from jax.sharding import PartitionSpec as P

VMEM = pl.BlockSpec(memory_space=pltpu.VMEM)
SMEM = pl.BlockSpec(memory_space=pltpu.SMEM)
LIMIT = 24 * 2**20


def exchange(x, axis, bit):
    count = lax.axis_size(axis)
    return lax.ppermute(x, axis, [(i, i ^ bit) for i in range(count)])


def bits_of(count):
    return [1 << n for n in range(count.bit_length() - 1)]


def split(x):
    high = x.astype(jnp.bfloat16)
    return high, (x - high.astype(jnp.float32)).astype(jnp.bfloat16)


def spread(row, copies):
    for i in range(copies.shape[0]):
        copies[i] = row[0]


def prepare(couplings, live, neighbours, energies, row, high, low, sources, diagonal):
    targets, slots = couplings.shape[0], couplings.shape[1]
    for i in range(targets):
        for n in range(slots):
            weight = live[i * slots + n].astype(jnp.float32)
            high[i, n], low[i, n] = split(couplings[i, n] * weight)
    sources[...] = neighbours[...]
    diagonal[...] = row[0] * energies[...]


def times(left, right):
    return lax.dot_general(
        left, right, (((1,), (1,)), ((), ())), preferred_element_type=jnp.float32
    )


def products(table, high, low, sources, diagonal, partial):
    targets, slots = high.shape[0], high.shape[1]
    vectors = table.shape[1]
    own_src = lax.axis_index("src")
    at = sources[...]
    for i in range(targets):
        total = None
        for n in range(slots):
            row = jnp.concatenate(split(table[at[i, n]]), axis=0)
            term = times(row, high[i, n]) + times(row, low[i, n])
            total = term if total is None else total + term
        partial[i] = total[:vectors] + total[vectors:]
    partial[own_src] = partial[own_src] + diagonal[...]


def contract(left, right):
    return lax.dot_general(
        left,
        right,
        (((1,), (1,)), ((), ())),
        precision=lax.Precision.HIGHEST,
        preferred_element_type=jnp.float32,
    )


def invert(table, out):
    rows, vectors, states = table.shape
    metric = jnp.zeros((vectors, vectors), jnp.float32)
    step = 32
    for r in range(0, rows, step):
        part = jnp.concatenate([table[i] for i in range(r, min(r + step, rows))], axis=1)
        metric = metric + contract(part, part)
    eye = (
        lax.broadcasted_iota(jnp.int32, (vectors, vectors), 0)
        == lax.broadcasted_iota(jnp.int32, (vectors, vectors), 1)
    )
    diagonal = jnp.sum(jnp.where(eye, metric, 0.0), axis=1, keepdims=True)
    sublane = lax.broadcasted_iota(jnp.int32, (vectors, states), 0)
    right = table[lax.axis_index("tgt") * lax.axis_size("src") + lax.axis_index("src")]
    wide = jnp.concatenate(
        [metric, jnp.where(eye, 1.0, 0.0), jnp.zeros((vectors, states - 2 * vectors), jnp.float32)],
        axis=1,
    )
    for j in range(vectors):
        column = wide[:, j : j + 1]
        inverse = 1.0 / wide[j : j + 1, j : j + 1]
        pivot = wide[j : j + 1, :] * inverse
        pivot_right = right[j : j + 1, :] * inverse
        wide = jnp.where(sublane == j, pivot, wide - column * pivot)
        right = jnp.where(sublane == j, pivot_right, right - column * pivot_right)
    out[0:vectors] = right
    out[vectors : 2 * vectors] = pltpu.roll(wide, states - vectors, 1)
    out[2 * vectors : 3 * vectors] = jnp.broadcast_to(diagonal, (vectors, states))


def grams(mine, theirs, table, own, gram, sigmas):
    targets, vectors, states = mine.shape
    first = lax.axis_index("tgt") * targets
    sigmas[...] = mine[...] + theirs[...]
    own[...] = sigmas[lax.axis_index("src")]
    block = jnp.concatenate([table[first + i] for i in range(targets)], axis=1)
    wide = jnp.concatenate([sigmas[i] for i in range(targets)], axis=1)
    small = contract(wide, jnp.concatenate([block, wide], axis=0))
    gram[...] = jnp.concatenate(
        [small, jnp.zeros((vectors, states - 2 * vectors), jnp.float32)], axis=1
    )


def finish(mine, theirs, solved, own, sigma, residual, norms):
    vectors, states = mine.shape
    gram = mine[...] + theirs[...]
    lane = lax.broadcasted_iota(jnp.int32, (vectors, states), 1)
    sublane = lax.broadcasted_iota(jnp.int32, (vectors, states), 0)
    left = own[...]
    sigma[0] = left
    mixing = jnp.zeros((vectors, states), jnp.float32)
    for j in range(vectors):
        column = gram[:, j : j + 1]
        left = left - column * solved[j : j + 1, :]
        mixing = mixing + column * solved[vectors + j : vectors + j + 1, :]
    residual[0] = left
    terms = jnp.where(lane == sublane + vectors, gram, 0.0) - jnp.where(
        lane < vectors, gram * mixing, 0.0
    )
    totals = jnp.sum(terms, axis=1, keepdims=True)
    column = jnp.sqrt(totals / solved[2 * vectors : 3 * vectors, :])
    norms[...] = jnp.sum(jnp.where(lane == sublane, column, 0.0), axis=0)[:vectors]


def shards(trial_vectors, couplings, neighbours, live_slots, energies):
    vectors, _, states = trial_vectors.shape
    targets = couplings.shape[0]
    src_count, tgt_count = lax.axis_size("src"), lax.axis_size("tgt")
    params = pltpu.CompilerParams(vmem_limit_bytes=LIMIT)

    def call(body, outs, in_specs, flops, moved, scratch=()):
        return pl.pallas_call(
            body,
            out_shape=outs,
            in_specs=in_specs,
            out_specs=jax.tree.map(lambda _: VMEM, outs),
            scratch_shapes=scratch,
            compiler_params=params,
            cost_estimate=pl.CostEstimate(
                flops=flops, bytes_accessed=moved, transcendentals=0
            ),
        )

    def shape(*dims, dtype=jnp.float32):
        return jax.ShapeDtypeStruct(dims, dtype)

    size = couplings.size
    row = jnp.transpose(trial_vectors, (1, 0, 2))
    copies = call(
        spread, shape(src_count * tgt_count, vectors, states), [VMEM], 0, 10**5
    )(row)
    high, low, sources, diagonal = call(
        prepare,
        (
            shape(*couplings.shape, dtype=jnp.bfloat16),
            shape(*couplings.shape, dtype=jnp.bfloat16),
            shape(*neighbours.shape, dtype=jnp.int32),
            shape(vectors, states),
        ),
        [VMEM, SMEM, VMEM, VMEM, VMEM],
        4 * size,
        8 * size,
    )(couplings, live_slots.reshape(-1), neighbours, energies, row)
    table = lax.all_to_all(copies, ("tgt", "src"), 0, 0, tiled=True)
    partial = call(
        products, shape(targets, vectors, states), [VMEM] * 5, 2 * size * vectors, 4 * size
    )(table, high, low, sources, diagonal)
    solved = call(invert, shape(3 * vectors, states), [VMEM], 10**6, 4 * table.size)(table)

    for bit in bits_of(src_count):
        theirs = exchange(partial, "src", bit)
        if 2 * bit < src_count:
            partial = partial + theirs
    own, gram = call(
        grams,
        (shape(vectors, states), shape(vectors, states)),
        [VMEM] * 3,
        10**6,
        12 * partial.size,
        [pltpu.VMEM((targets, vectors, states), jnp.float32)],
    )(partial, theirs, table)

    for bit in reversed(bits_of(tgt_count)):
        theirs = exchange(gram, "tgt", bit)
        if bit > 1:
            gram = gram + theirs
    sigma, residual, norms = call(
        finish,
        (shape(1, vectors, states), shape(1, vectors, states), shape(vectors)),
        [VMEM] * 4,
        10**4,
        10**5,
    )(gram, theirs, solved, own)
    return (jnp.transpose(sigma, (1, 0, 2)), jnp.transpose(residual, (1, 0, 2)), norms)


def solution(mesh):
    return jax.shard_map(
        shards,
        mesh=mesh,
        in_specs=(
            P(None, ("tgt", "src"), None),
            P("tgt", "src", None, None),
            P("tgt", "src"),
            P("tgt", "src"),
            P(("tgt", "src"), None),
        ),
        out_specs=(P(None, ("tgt", "src"), None), P(None, ("tgt", "src"), None), P()),
        check_vma=False,
    )
```

```python
import jax
import jax.numpy as jnp
from jax import lax
from jax.experimental import pallas as pl
from jax.experimental.pallas import tpu as pltpu
from jax.sharding import PartitionSpec as P

VMEM = pl.BlockSpec(memory_space=pltpu.VMEM)
SMEM = pl.BlockSpec(memory_space=pltpu.SMEM)
LIMIT = 24 * 2**20


def exchange(x, axis, bit):
    count = lax.axis_size(axis)
    return lax.ppermute(x, axis, [(i, i ^ bit) for i in range(count)])


def bits_of(count):
    return [1 << n for n in range(count.bit_length() - 1)]


def split(x):
    high = x.astype(jnp.bfloat16)
    return high, (x - high.astype(jnp.float32)).astype(jnp.bfloat16)


def spread(row, copies, own, filled, sem):
    move = pltpu.make_async_copy(row, own, sem)
    move.start()
    move.wait()
    for i in range(filled.shape[0]):
        filled[i] = own[0]
    move = pltpu.make_async_copy(filled, copies, sem)
    move.start()
    move.wait()


def prepare(couplings, live, neighbours, energies, row, high, low, sources, diagonal):
    targets, slots = couplings.shape[0], couplings.shape[1]
    for i in range(targets):
        for n in range(slots):
            weight = live[i * slots + n].astype(jnp.float32)
            high[i, n], low[i, n] = split(couplings[i, n] * weight)
    sources[...] = neighbours[...]
    diagonal[...] = row[0] * energies[...]


def times(left, right):
    return lax.dot_general(
        left, right, (((1,), (1,)), ((), ())), preferred_element_type=jnp.float32
    )


def products(table, high, low, sources, diagonal, partial):
    targets, slots = high.shape[0], high.shape[1]
    vectors = table.shape[1]
    own_src = lax.axis_index("src")
    at = sources[...]
    for i in range(targets):
        total = None
        for n in range(slots):
            row = jnp.concatenate(split(table[at[i, n]]), axis=0)
            term = times(row, high[i, n]) + times(row, low[i, n])
            total = term if total is None else total + term
        partial[i] = total[:vectors] + total[vectors:]
    partial[own_src] = partial[own_src] + diagonal[...]


def contract(left, right):
    return lax.dot_general(
        left,
        right,
        (((1,), (1,)), ((), ())),
        precision=lax.Precision.HIGHEST,
        preferred_element_type=jnp.float32,
    )


def invert(table, out):
    rows, vectors, states = table.shape
    metric = jnp.zeros((vectors, vectors), jnp.float32)
    step = 32
    for r in range(0, rows, step):
        part = jnp.concatenate([table[i] for i in range(r, min(r + step, rows))], axis=1)
        metric = metric + contract(part, part)
    eye = (
        lax.broadcasted_iota(jnp.int32, (vectors, vectors), 0)
        == lax.broadcasted_iota(jnp.int32, (vectors, vectors), 1)
    )
    diagonal = jnp.sum(jnp.where(eye, metric, 0.0), axis=1, keepdims=True)
    sublane = lax.broadcasted_iota(jnp.int32, (vectors, states), 0)
    right = table[lax.axis_index("tgt") * lax.axis_size("src") + lax.axis_index("src")]
    wide = jnp.concatenate(
        [metric, jnp.where(eye, 1.0, 0.0), jnp.zeros((vectors, states - 2 * vectors), jnp.float32)],
        axis=1,
    )
    for j in range(vectors):
        column = wide[:, j : j + 1]
        inverse = 1.0 / wide[j : j + 1, j : j + 1]
        pivot = wide[j : j + 1, :] * inverse
        pivot_right = right[j : j + 1, :] * inverse
        wide = jnp.where(sublane == j, pivot, wide - column * pivot)
        right = jnp.where(sublane == j, pivot_right, right - column * pivot_right)
    out[0:vectors] = right
    out[vectors : 2 * vectors] = pltpu.roll(wide, states - vectors, 1)
    out[2 * vectors : 3 * vectors] = jnp.broadcast_to(diagonal, (vectors, states))


def grams(mine, theirs, table, own, gram, sigmas):
    targets, vectors, states = mine.shape
    first = lax.axis_index("tgt") * targets
    sigmas[...] = mine[...] + theirs[...]
    own[...] = sigmas[lax.axis_index("src")]
    block = jnp.concatenate([table[first + i] for i in range(targets)], axis=1)
    wide = jnp.concatenate([sigmas[i] for i in range(targets)], axis=1)
    small = contract(wide, jnp.concatenate([block, wide], axis=0))
    gram[...] = jnp.concatenate(
        [small, jnp.zeros((vectors, states - 2 * vectors), jnp.float32)], axis=1
    )


def finish(*refs):
    pieces, (solved, own, sigma, residual, norms) = refs[:-5], refs[-5:]
    vectors, states = own.shape
    gram = pieces[0][...]
    for piece in pieces[1:]:
        gram = gram + piece[...]
    lane = lax.broadcasted_iota(jnp.int32, (vectors, states), 1)
    sublane = lax.broadcasted_iota(jnp.int32, (vectors, states), 0)
    left = own[...]
    sigma[0] = left
    mixing = jnp.zeros((vectors, states), jnp.float32)
    for j in range(vectors):
        column = gram[:, j : j + 1]
        left = left - column * solved[j : j + 1, :]
        mixing = mixing + column * solved[vectors + j : vectors + j + 1, :]
    residual[0] = left
    terms = jnp.where(lane == sublane + vectors, gram, 0.0) - jnp.where(
        lane < vectors, gram * mixing, 0.0
    )
    totals = jnp.sum(terms, axis=1, keepdims=True)
    column = jnp.sqrt(totals / solved[2 * vectors : 3 * vectors, :])
    norms[...] = jnp.sum(jnp.where(lane == sublane, column, 0.0), axis=0)[:vectors]


def shards(trial_vectors, couplings, neighbours, live_slots, energies):
    vectors, _, states = trial_vectors.shape
    targets = couplings.shape[0]
    src_count, tgt_count = lax.axis_size("src"), lax.axis_size("tgt")
    params = pltpu.CompilerParams(vmem_limit_bytes=LIMIT)

    def call(body, outs, in_specs, flops, moved, scratch=()):
        return pl.pallas_call(
            body,
            out_shape=outs,
            in_specs=in_specs,
            out_specs=jax.tree.map(lambda _: VMEM, outs),
            scratch_shapes=scratch,
            compiler_params=params,
            cost_estimate=pl.CostEstimate(
                flops=flops, bytes_accessed=moved, transcendentals=0
            ),
        )

    def shape(*dims, dtype=jnp.float32):
        return jax.ShapeDtypeStruct(dims, dtype)

    size = couplings.size
    row = jnp.transpose(trial_vectors, (1, 0, 2))
    count = src_count * tgt_count
    copies = pl.pallas_call(
        spread,
        out_shape=shape(count, vectors, states),
        in_specs=[pl.BlockSpec(memory_space=pl.ANY)],
        out_specs=pl.BlockSpec(memory_space=pl.ANY),
        scratch_shapes=[
            pltpu.VMEM(row.shape, jnp.float32),
            pltpu.VMEM((count, vectors, states), jnp.float32),
            pltpu.SemaphoreType.DMA(()),
        ],
    )(row)
    high, low, sources, diagonal = call(
        prepare,
        (
            shape(*couplings.shape, dtype=jnp.bfloat16),
            shape(*couplings.shape, dtype=jnp.bfloat16),
            shape(*neighbours.shape, dtype=jnp.int32),
            shape(vectors, states),
        ),
        [VMEM, SMEM, VMEM, VMEM, VMEM],
        4 * size,
        8 * size,
    )(couplings, live_slots.reshape(-1), neighbours, energies, row)
    table = lax.all_to_all(copies, ("tgt", "src"), 0, 0, tiled=True)
    partial = call(
        products, shape(targets, vectors, states), [VMEM] * 5, 2 * size * vectors, 4 * size
    )(table, high, low, sources, diagonal)
    solved = call(invert, shape(3 * vectors, states), [VMEM], 10**6, 4 * table.size)(table)

    for bit in bits_of(src_count):
        theirs = exchange(partial, "src", bit)
        if 2 * bit < src_count:
            partial = partial + theirs
            partial, solved = lax.optimization_barrier((partial, solved))
    own, gram = call(
        grams,
        (shape(vectors, states), shape(vectors, states)),
        [VMEM] * 3,
        10**6,
        12 * partial.size,
        [pltpu.VMEM((targets, vectors, states), jnp.float32)],
    )(partial, theirs, table)

    for bit in reversed(bits_of(tgt_count)[2:]):
        gram = gram + exchange(gram, "tgt", bit)
    pieces = [gram] + [exchange(gram, "tgt", bit) for bit in reversed(range(1, min(tgt_count, 4)))]
    sigma, residual, norms = call(
        finish,
        (shape(1, vectors, states), shape(1, vectors, states), shape(vectors)),
        [VMEM] * (len(pieces) + 2),
        10**4,
        10**5,
    )(*pieces, solved, own)
    return (jnp.transpose(sigma, (1, 0, 2)), jnp.transpose(residual, (1, 0, 2)), norms)


def solution(mesh):
    return jax.shard_map(
        shards,
        mesh=mesh,
        in_specs=(
            P(None, ("tgt", "src"), None),
            P("tgt", "src", None, None),
            P("tgt", "src"),
            P("tgt", "src"),
            P(("tgt", "src"), None),
        ),
        out_specs=(P(None, ("tgt", "src"), None), P(None, ("tgt", "src"), None), P()),
        check_vma=False,
    )
```

```python
import jax
import jax.numpy as jnp
from jax import lax
from jax.experimental import pallas as pl
from jax.experimental.pallas import tpu as pltpu
from jax.sharding import PartitionSpec as P

VMEM = pl.BlockSpec(memory_space=pltpu.VMEM)
LIMIT = 24 * 2**20


def exchange(x, axis, bit):
    count = lax.axis_size(axis)
    return lax.ppermute(x, axis, [(i, i ^ bit) for i in range(count)])


def pair(x, bits):
    tgt_count, src_count = lax.axis_size("tgt"), lax.axis_size("src")
    partners = [
        (t * src_count + s, t * src_count + (s ^ bits[t % 2]))
        for t in range(tgt_count)
        for s in range(src_count)
    ]
    return lax.ppermute(x, ("tgt", "src"), partners)


def bits_of(count):
    return [1 << n for n in range(count.bit_length() - 1)]


def split(x):
    high = x.astype(jnp.bfloat16)
    return high, (x - high.astype(jnp.float32)).astype(jnp.bfloat16)


def spread(row, neighbours, live, energies, copies, side, own, at, alive, energy, filled, packed, sems):
    slots, targets = live.shape
    vectors = own.shape[1]
    inward = [
        pltpu.make_async_copy(source, target, sems.at[n])
        for n, (source, target) in enumerate(
            [(row, own), (neighbours, at), (live, alive), (energies, energy)]
        )
    ]
    for move in inward:
        move.start()
    inward[0].wait()
    for i in range(filled.shape[0]):
        filled[i] = own[0]
    outward = pltpu.make_async_copy(filled, copies, sems.at[0])
    outward.start()
    for move in inward[1:]:
        move.wait()
    packed[...] = jnp.zeros_like(packed)
    packed[0:vectors] = own[0] * energy[...]
    packed[vectors : vectors + slots, 0:targets] = at[...].astype(jnp.float32)
    packed[vectors + slots : vectors + 2 * slots, 0:targets] = alive[...].astype(jnp.float32)
    sent = pltpu.make_async_copy(packed, side, sems.at[1])
    sent.start()
    outward.wait()
    sent.wait()


def prepare(couplings, side, halves):
    targets, slots, states = couplings.shape[:3]
    first = side.shape[0] - slots
    for i in range(targets):
        for n in range(slots):
            weight = side[first + n : first + n + 1, i : i + 1]
            halves[i, n, :states], halves[i, n, states:] = split(couplings[i, n] * weight)


def times(left, right):
    return lax.dot_general(
        left, right, (((1,), (1,)), ((), ())), preferred_element_type=jnp.float32
    )


def products(table, halves, side, other_halves, other_side, partial):
    targets, slots = halves.shape[0], halves.shape[1]
    vectors, states = table.shape[1:]
    own_src = lax.axis_index("src")
    away = 1 + lax.axis_index("tgt") % 2
    at = side[vectors : vectors + slots].astype(jnp.int32)
    other_at = other_side[vectors : vectors + slots].astype(jnp.int32)
    for i in range(targets):
        total = None
        for n in range(slots):
            rows = jnp.concatenate([table[at[n, i]], table[other_at[n, i]]], axis=1)
            term = times(
                jnp.concatenate(split(rows), axis=0),
                jnp.concatenate([halves[i, n], other_halves[i, n]], axis=1),
            )
            total = term if total is None else total + term
        total = total[:, :states] + total[:, states:]
        partial[i] = total[:vectors] + total[vectors:]
    partial[own_src] = partial[own_src] + side[0:vectors]
    partial[own_src ^ away] = partial[own_src ^ away] + other_side[0:vectors]


def contract(left, right):
    return lax.dot_general(
        left,
        right,
        (((1,), (1,)), ((), ())),
        precision=lax.Precision.HIGHEST,
        preferred_element_type=jnp.float32,
    )


def invert(table, out):
    rows, vectors, states = table.shape
    metric = jnp.zeros((vectors, vectors), jnp.float32)
    step = 32
    for r in range(0, rows, step):
        part = jnp.concatenate([table[i] for i in range(r, min(r + step, rows))], axis=1)
        metric = metric + contract(part, part)
    eye = (
        lax.broadcasted_iota(jnp.int32, (vectors, vectors), 0)
        == lax.broadcasted_iota(jnp.int32, (vectors, vectors), 1)
    )
    diagonal = jnp.sum(jnp.where(eye, metric, 0.0), axis=1, keepdims=True)
    sublane = lax.broadcasted_iota(jnp.int32, (vectors, states), 0)
    right = table[lax.axis_index("tgt") * lax.axis_size("src") + lax.axis_index("src")]
    wide = jnp.concatenate(
        [metric, jnp.where(eye, 1.0, 0.0), jnp.zeros((vectors, states - 2 * vectors), jnp.float32)],
        axis=1,
    )
    for j in range(vectors):
        column = wide[:, j : j + 1]
        inverse = 1.0 / wide[j : j + 1, j : j + 1]
        pivot = wide[j : j + 1, :] * inverse
        pivot_right = right[j : j + 1, :] * inverse
        wide = jnp.where(sublane == j, pivot, wide - column * pivot)
        right = jnp.where(sublane == j, pivot_right, right - column * pivot_right)
    out[0:vectors] = right
    out[vectors : 2 * vectors] = pltpu.roll(wide, states - vectors, 1)
    out[2 * vectors : 3 * vectors] = jnp.broadcast_to(diagonal, (vectors, states))


def grams(mine, theirs, table, own, gram, sigmas):
    targets, vectors, states = mine.shape
    first = lax.axis_index("tgt") * targets
    sigmas[...] = mine[...] + theirs[...]
    own[...] = sigmas[lax.axis_index("src")]
    block = jnp.concatenate([table[first + i] for i in range(targets)], axis=1)
    wide = jnp.concatenate([sigmas[i] for i in range(targets)], axis=1)
    small = contract(wide, jnp.concatenate([block, wide], axis=0))
    gram[...] = jnp.concatenate(
        [small, jnp.zeros((vectors, states - 2 * vectors), jnp.float32)], axis=1
    )


def finish(*refs):
    pieces, (solved, own, sigma, residual, norms) = refs[:-5], refs[-5:]
    vectors, states = own.shape
    pieces = [piece[...] for piece in pieces]
    while len(pieces) > 1:
        pieces = [left + right for left, right in zip(pieces[::2], pieces[1::2])]
    gram = pieces[0]
    lane = lax.broadcasted_iota(jnp.int32, (vectors, states), 1)
    sublane = lax.broadcasted_iota(jnp.int32, (vectors, states), 0)
    left = own[...]
    sigma[0] = left
    mixing = jnp.zeros((vectors, states), jnp.float32)
    for j in range(vectors):
        column = gram[:, j : j + 1]
        left = left - column * solved[j : j + 1, :]
        mixing = mixing + column * solved[vectors + j : vectors + j + 1, :]
    residual[0] = left
    terms = jnp.where(lane == sublane + vectors, gram, 0.0) - jnp.where(
        lane < vectors, gram * mixing, 0.0
    )
    totals = jnp.sum(terms, axis=1, keepdims=True)
    column = jnp.sqrt(totals / solved[2 * vectors : 3 * vectors, :])
    norms[...] = jnp.sum(jnp.where(lane == sublane, column, 0.0), axis=0)[:vectors]


def shards(trial_vectors, couplings, neighbours, live_slots, energies):
    vectors, _, states = trial_vectors.shape
    targets = couplings.shape[0]
    src_count, tgt_count = lax.axis_size("src"), lax.axis_size("tgt")
    params = pltpu.CompilerParams(vmem_limit_bytes=LIMIT)

    def call(body, outs, in_specs, flops, moved, scratch=()):
        return pl.pallas_call(
            body,
            out_shape=outs,
            in_specs=in_specs,
            out_specs=jax.tree.map(lambda _: VMEM, outs),
            scratch_shapes=scratch,
            compiler_params=params,
            cost_estimate=pl.CostEstimate(
                flops=flops, bytes_accessed=moved, transcendentals=0
            ),
        )

    def shape(*dims, dtype=jnp.float32):
        return jax.ShapeDtypeStruct(dims, dtype)

    size = couplings.size
    row = jnp.transpose(trial_vectors, (1, 0, 2))
    count, slots = src_count * tgt_count, couplings.shape[1]
    side_shape = (vectors + 2 * slots, states)
    anywhere = pl.BlockSpec(memory_space=pl.ANY)
    copies, side = pl.pallas_call(
        spread,
        out_shape=(shape(count, vectors, states), shape(*side_shape)),
        in_specs=[anywhere] * 4,
        out_specs=[anywhere] * 2,
        scratch_shapes=[
            pltpu.VMEM(row.shape, jnp.float32),
            pltpu.VMEM((slots, targets), jnp.int32),
            pltpu.VMEM((slots, targets), jnp.int32),
            pltpu.VMEM(energies.shape, jnp.float32),
            pltpu.VMEM((count, vectors, states), jnp.float32),
            pltpu.VMEM(side_shape, jnp.float32),
            pltpu.SemaphoreType.DMA((4,)),
        ],
    )(row, neighbours.T, live_slots.T, energies)
    other_side = pair(side, (1, 2))
    other = pair(couplings, (1, 2))
    half = shape(targets, slots, 2 * states, states, dtype=jnp.bfloat16)
    halve = call(prepare, half, [VMEM] * 2, 4 * size, 8 * size)
    halves, other_halves = halve(couplings, side), halve(other, other_side)
    table = lax.all_to_all(copies, ("tgt", "src"), 0, 0, tiled=True)
    partial = call(
        products, shape(targets, vectors, states), [VMEM] * 5, 4 * size * vectors, 8 * size
    )(table, halves, side, other_halves, other_side)
    solved = call(invert, shape(3 * vectors, states), [VMEM], 10**6, 4 * table.size)(table)

    steps = [(2, 1)] + [(bit, bit) for bit in bits_of(src_count)[2:]]
    for n, step in enumerate(steps):
        theirs = pair(partial, step)
        if n + 1 < len(steps):
            partial = partial + theirs
            partial, solved = lax.optimization_barrier((partial, solved))
    own, gram = call(
        grams,
        (shape(vectors, states), shape(vectors, states)),
        [VMEM] * 3,
        10**6,
        12 * partial.size,
        [pltpu.VMEM((targets, vectors, states), jnp.float32)],
    )(partial, theirs, table)

    for bit in reversed(bits_of(tgt_count)[2:]):
        gram = gram + exchange(gram, "tgt", bit)
    pieces = [exchange(gram, "tgt", bit) for bit in reversed(range(1, min(tgt_count, 4)))]
    pieces = pieces + [gram]
    sigma, residual, norms = call(
        finish,
        (shape(1, vectors, states), shape(1, vectors, states), shape(vectors)),
        [VMEM] * (len(pieces) + 2),
        10**4,
        10**5,
    )(*pieces, solved, own)
    return (jnp.transpose(sigma, (1, 0, 2)), jnp.transpose(residual, (1, 0, 2)), norms)


def solution(mesh):
    return jax.shard_map(
        shards,
        mesh=mesh,
        in_specs=(
            P(None, ("tgt", "src"), None),
            P("tgt", "src", None, None),
            P("tgt", "src"),
            P("tgt", "src"),
            P(("tgt", "src"), None),
        ),
        out_specs=(P(None, ("tgt", "src"), None), P(None, ("tgt", "src"), None), P()),
        check_vma=False,
    )
```

```python
import jax
import jax.numpy as jnp
from jax import lax
from jax.experimental import pallas as pl
from jax.experimental.pallas import tpu as pltpu
from jax.sharding import PartitionSpec as P

VMEM = pl.BlockSpec(memory_space=pltpu.VMEM)
LIMIT = 24 * 2**20


def exchange(x, axis, bit):
    count = lax.axis_size(axis)
    return lax.ppermute(x, axis, [(i, i ^ bit) for i in range(count)])


def pair(x, bits):
    tgt_count, src_count = lax.axis_size("tgt"), lax.axis_size("src")
    partners = [
        (t * src_count + s, t * src_count + (s ^ bits[t % 2]))
        for t in range(tgt_count)
        for s in range(src_count)
    ]
    return lax.ppermute(x, ("tgt", "src"), partners)


def bits_of(count):
    return [1 << n for n in range(count.bit_length() - 1)]


def split(x):
    high = x.astype(jnp.bfloat16)
    return high, (x - high.astype(jnp.float32)).astype(jnp.bfloat16)


def spread(row, neighbours, live, energies, copies, side, own, at, alive, energy, filled, packed, sems):
    slots, targets = live.shape
    vectors = own.shape[1]
    inward = [
        pltpu.make_async_copy(source, target, sems.at[n])
        for n, (source, target) in enumerate(
            [(row, own), (neighbours, at), (live, alive), (energies, energy)]
        )
    ]
    for move in inward:
        move.start()
    inward[0].wait()
    for i in range(filled.shape[0]):
        filled[i] = own[0]
    outward = pltpu.make_async_copy(filled, copies, sems.at[0])
    outward.start()
    for move in inward[1:]:
        move.wait()
    packed[...] = jnp.zeros_like(packed)
    packed[0:vectors] = own[0] * energy[...]
    packed[vectors : vectors + slots, 0:targets] = at[...].astype(jnp.float32)
    packed[vectors + slots : vectors + 2 * slots, 0:targets] = alive[...].astype(jnp.float32)
    sent = pltpu.make_async_copy(packed, side, sems.at[1])
    sent.start()
    outward.wait()
    sent.wait()


def prepare(couplings, side, halves):
    targets, slots, states = couplings.shape[:3]
    first = side.shape[0] - slots
    for i in range(targets):
        for n in range(slots):
            weight = side[first + n : first + n + 1, i : i + 1]
            halves[i, n, :states], halves[i, n, states:] = split(couplings[i, n] * weight)


def times(left, right):
    return lax.dot_general(
        left, right, (((1,), (1,)), ((), ())), preferred_element_type=jnp.float32
    )


def products(table, halves, side, other_halves, other_side, partial):
    targets, slots = halves.shape[0], halves.shape[1]
    vectors, states = table.shape[1:]
    own_src = lax.axis_index("src")
    away = 1 + lax.axis_index("tgt") % 2
    at = side[vectors : vectors + slots].astype(jnp.int32)
    other_at = other_side[vectors : vectors + slots].astype(jnp.int32)
    for i in range(targets):
        total = None
        for n in range(slots):
            rows = jnp.concatenate([table[at[n, i]], table[other_at[n, i]]], axis=1)
            term = times(
                jnp.concatenate(split(rows), axis=0),
                jnp.concatenate([halves[i, n], other_halves[i, n]], axis=1),
            )
            total = term if total is None else total + term
        total = total[:, :states] + total[:, states:]
        partial[i] = total[:vectors] + total[vectors:]
    partial[own_src] = partial[own_src] + side[0:vectors]
    partial[own_src ^ away] = partial[own_src ^ away] + other_side[0:vectors]


def contract(left, right):
    return lax.dot_general(
        left,
        right,
        (((1,), (1,)), ((), ())),
        precision=lax.Precision.HIGHEST,
        preferred_element_type=jnp.float32,
    )


def invert(table, out):
    rows, vectors, states = table.shape
    metric = jnp.zeros((vectors, vectors), jnp.float32)
    step = 32
    for r in range(0, rows, step):
        part = jnp.concatenate([table[i] for i in range(r, min(r + step, rows))], axis=1)
        metric = metric + contract(part, part)
    eye = (
        lax.broadcasted_iota(jnp.int32, (vectors, vectors), 0)
        == lax.broadcasted_iota(jnp.int32, (vectors, vectors), 1)
    )
    diagonal = jnp.sum(jnp.where(eye, metric, 0.0), axis=1, keepdims=True)
    sublane = lax.broadcasted_iota(jnp.int32, (vectors, states), 0)
    right = table[lax.axis_index("tgt") * lax.axis_size("src") + lax.axis_index("src")]
    wide = jnp.concatenate(
        [metric, jnp.where(eye, 1.0, 0.0), jnp.zeros((vectors, states - 2 * vectors), jnp.float32)],
        axis=1,
    )
    for j in range(vectors):
        column = wide[:, j : j + 1]
        inverse = 1.0 / wide[j : j + 1, j : j + 1]
        pivot = wide[j : j + 1, :] * inverse
        pivot_right = right[j : j + 1, :] * inverse
        wide = jnp.where(sublane == j, pivot, wide - column * pivot)
        right = jnp.where(sublane == j, pivot_right, right - column * pivot_right)
    out[0:vectors] = right
    out[vectors : 2 * vectors] = pltpu.roll(wide, states - vectors, 1)
    out[2 * vectors : 3 * vectors] = jnp.broadcast_to(diagonal, (vectors, states))


def grams(mine, theirs, table, own, gram, sigmas):
    targets, vectors, states = mine.shape
    first = lax.axis_index("tgt") * targets
    sigmas[...] = mine[...] + theirs[...]
    own[...] = sigmas[lax.axis_index("src")]
    block = jnp.concatenate([table[first + i] for i in range(targets)], axis=1)
    wide = jnp.concatenate([sigmas[i] for i in range(targets)], axis=1)
    small = contract(wide, jnp.concatenate([block, wide], axis=0))
    gram[...] = jnp.concatenate(
        [small, jnp.zeros((vectors, states - 2 * vectors), jnp.float32)], axis=1
    )


def finish(*refs):
    pieces, (solved, own, sigma, residual, norms) = refs[:-5], refs[-5:]
    vectors, states = own.shape
    pieces = [piece[...] for piece in pieces]
    while len(pieces) > 1:
        pieces = [left + right for left, right in zip(pieces[::2], pieces[1::2])]
    gram = pieces[0]
    lane = lax.broadcasted_iota(jnp.int32, (vectors, states), 1)
    sublane = lax.broadcasted_iota(jnp.int32, (vectors, states), 0)
    left = own[...]
    sigma[0] = left
    mixing = jnp.zeros((vectors, states), jnp.float32)
    for j in range(vectors):
        column = gram[:, j : j + 1]
        left = left - column * solved[j : j + 1, :]
        mixing = mixing + column * solved[vectors + j : vectors + j + 1, :]
    residual[0] = left
    terms = jnp.where(lane == sublane + vectors, gram, 0.0) - jnp.where(
        lane < vectors, gram * mixing, 0.0
    )
    totals = jnp.maximum(jnp.sum(terms, axis=1, keepdims=True), 0.0)
    column = jnp.sqrt(totals / solved[2 * vectors : 3 * vectors, :])
    norms[...] = jnp.sum(jnp.where(lane == sublane, column, 0.0), axis=0)[:vectors]


def shards(trial_vectors, couplings, neighbours, live_slots, energies):
    vectors, _, states = trial_vectors.shape
    targets = couplings.shape[0]
    src_count, tgt_count = lax.axis_size("src"), lax.axis_size("tgt")
    params = pltpu.CompilerParams(vmem_limit_bytes=LIMIT)

    def call(body, outs, in_specs, flops, moved, scratch=()):
        return pl.pallas_call(
            body,
            out_shape=outs,
            in_specs=in_specs,
            out_specs=jax.tree.map(lambda _: VMEM, outs),
            scratch_shapes=scratch,
            compiler_params=params,
            cost_estimate=pl.CostEstimate(
                flops=flops, bytes_accessed=moved, transcendentals=0
            ),
        )

    def shape(*dims, dtype=jnp.float32):
        return jax.ShapeDtypeStruct(dims, dtype)

    size = couplings.size
    row = jnp.transpose(trial_vectors, (1, 0, 2))
    count, slots = src_count * tgt_count, couplings.shape[1]
    side_shape = (vectors + 2 * slots, states)
    anywhere = pl.BlockSpec(memory_space=pl.ANY)
    copies, side = pl.pallas_call(
        spread,
        out_shape=(shape(count, vectors, states), shape(*side_shape)),
        in_specs=[anywhere] * 4,
        out_specs=[anywhere] * 2,
        scratch_shapes=[
            pltpu.VMEM(row.shape, jnp.float32),
            pltpu.VMEM((slots, targets), jnp.int32),
            pltpu.VMEM((slots, targets), jnp.int32),
            pltpu.VMEM(energies.shape, jnp.float32),
            pltpu.VMEM((count, vectors, states), jnp.float32),
            pltpu.VMEM(side_shape, jnp.float32),
            pltpu.SemaphoreType.DMA((4,)),
        ],
    )(row, neighbours.T, live_slots.T, energies)
    other_side = pair(side, (1, 2))
    other = pair(couplings, (1, 2))
    half = shape(targets, slots, 2 * states, states, dtype=jnp.bfloat16)
    halve = call(prepare, half, [VMEM] * 2, 4 * size, 8 * size)
    halves, other_halves = halve(couplings, side), halve(other, other_side)
    table = lax.all_to_all(copies, ("tgt", "src"), 0, 0, tiled=True)
    partial = call(
        products, shape(targets, vectors, states), [VMEM] * 5, 4 * size * vectors, 8 * size
    )(table, halves, side, other_halves, other_side)
    solved = call(invert, shape(3 * vectors, states), [VMEM], 10**6, 4 * table.size)(table)

    steps = [(2, 1)] + [(bit, bit) for bit in bits_of(src_count)[2:]]
    for n, step in enumerate(steps):
        theirs = pair(partial, step)
        if n + 1 < len(steps):
            partial = partial + theirs
            partial, solved = lax.optimization_barrier((partial, solved))
    own, gram = call(
        grams,
        (shape(vectors, states), shape(vectors, states)),
        [VMEM] * 3,
        10**6,
        12 * partial.size,
        [pltpu.VMEM((targets, vectors, states), jnp.float32)],
    )(partial, theirs, table)

    for bit in reversed(bits_of(tgt_count)[2:]):
        gram = gram + exchange(gram, "tgt", bit)
    pieces = [exchange(gram, "tgt", bit) for bit in reversed(range(1, min(tgt_count, 4)))]
    pieces = pieces + [gram]
    sigma, residual, norms = call(
        finish,
        (shape(1, vectors, states), shape(1, vectors, states), shape(vectors)),
        [VMEM] * (len(pieces) + 2),
        10**4,
        10**5,
    )(*pieces, solved, own)
    return (jnp.transpose(sigma, (1, 0, 2)), jnp.transpose(residual, (1, 0, 2)), norms)


def solution(mesh):
    return jax.shard_map(
        shards,
        mesh=mesh,
        in_specs=(
            P(None, ("tgt", "src"), None),
            P("tgt", "src", None, None),
            P("tgt", "src"),
            P("tgt", "src"),
            P(("tgt", "src"), None),
        ),
        out_specs=(P(None, ("tgt", "src"), None), P(None, ("tgt", "src"), None), P()),
        check_vma=False,
    )
```

```python
import jax
import jax.numpy as jnp
from jax import lax
from jax.experimental import pallas as pl
from jax.experimental.pallas import tpu as pltpu
from jax.sharding import PartitionSpec as P

VMEM = pl.BlockSpec(memory_space=pltpu.VMEM)
LIMIT = 24 * 2**20


def exchange(x, axis, bit):
    count = lax.axis_size(axis)
    return lax.ppermute(x, axis, [(i, i ^ bit) for i in range(count)])


def pair(x, bits):
    tgt_count, src_count = lax.axis_size("tgt"), lax.axis_size("src")
    partners = [
        (t * src_count + s, t * src_count + (s ^ bits[t % 2]))
        for t in range(tgt_count)
        for s in range(src_count)
    ]
    return lax.ppermute(x, ("tgt", "src"), partners)


def bits_of(count):
    return [1 << n for n in range(count.bit_length() - 1)]


def split(x):
    high = x.astype(jnp.bfloat16)
    return high, (x - high.astype(jnp.float32)).astype(jnp.bfloat16)


def spread(row, neighbours, live, energies, copies, side, own, at, alive, energy, filled, packed, sems):
    slots, targets = live.shape
    vectors = own.shape[1]
    inward = [
        pltpu.make_async_copy(source, target, sems.at[n])
        for n, (source, target) in enumerate(
            [(row, own), (neighbours, at), (live, alive), (energies, energy)]
        )
    ]
    for move in inward:
        move.start()
    inward[0].wait()
    for i in range(filled.shape[0]):
        filled[i] = own[0]
    outward = pltpu.make_async_copy(filled, copies, sems.at[0])
    outward.start()
    for move in inward[1:]:
        move.wait()
    packed[...] = jnp.zeros_like(packed)
    packed[0:vectors] = own[0] * energy[...]
    packed[vectors : vectors + slots, 0:targets] = at[...].astype(jnp.float32)
    packed[vectors + slots : vectors + 2 * slots, 0:targets] = alive[...].astype(jnp.float32)
    sent = pltpu.make_async_copy(packed, side, sems.at[1])
    sent.start()
    outward.wait()
    sent.wait()


def prepare(couplings, side, halves):
    targets, slots, states = couplings.shape[:3]
    first = side.shape[0] - slots
    for i in range(targets):
        for n in range(slots):
            weight = side[first + n : first + n + 1, i : i + 1]
            halves[i, n, :states], halves[i, n, states:] = split(couplings[i, n] * weight)


def times(left, right):
    return lax.dot_general(
        left, right, (((1,), (1,)), ((), ())), preferred_element_type=jnp.float32
    )


def products(table, halves, side, other_halves, other_side, partial):
    targets, slots = halves.shape[0], halves.shape[1]
    vectors, states = table.shape[1:]
    own_src = lax.axis_index("src")
    away = 1 + lax.axis_index("tgt") % 2
    at = side[vectors : vectors + slots].astype(jnp.int32)
    other_at = other_side[vectors : vectors + slots].astype(jnp.int32)
    for i in range(targets):
        total = None
        for n in range(slots):
            rows = jnp.concatenate([table[at[n, i]], table[other_at[n, i]]], axis=1)
            term = times(
                jnp.concatenate(split(rows), axis=0),
                jnp.concatenate([halves[i, n], other_halves[i, n]], axis=1),
            )
            total = term if total is None else total + term
        total = total[:, :states] + total[:, states:]
        partial[i] = total[:vectors] + total[vectors:]
    partial[own_src] = partial[own_src] + side[0:vectors]
    partial[own_src ^ away] = partial[own_src ^ away] + other_side[0:vectors]


def contract(left, right):
    return lax.dot_general(
        left,
        right,
        (((1,), (1,)), ((), ())),
        precision=lax.Precision.HIGHEST,
        preferred_element_type=jnp.float32,
    )


def invert(table, out):
    rows, vectors, states = table.shape
    metric = jnp.zeros((vectors, vectors), jnp.float32)
    step = 32
    for r in range(0, rows, step):
        part = jnp.concatenate([table[i] for i in range(r, min(r + step, rows))], axis=1)
        metric = metric + contract(part, part)
    eye = (
        lax.broadcasted_iota(jnp.int32, (vectors, vectors), 0)
        == lax.broadcasted_iota(jnp.int32, (vectors, vectors), 1)
    )
    diagonal = jnp.sum(jnp.where(eye, metric, 0.0), axis=1, keepdims=True)
    sublane = lax.broadcasted_iota(jnp.int32, (vectors, states), 0)
    right = table[lax.axis_index("tgt") * lax.axis_size("src") + lax.axis_index("src")]
    wide = jnp.concatenate(
        [metric, jnp.where(eye, 1.0, 0.0), jnp.zeros((vectors, states - 2 * vectors), jnp.float32)],
        axis=1,
    )
    for j in range(vectors):
        column = wide[:, j : j + 1]
        inverse = 1.0 / wide[j : j + 1, j : j + 1]
        pivot = wide[j : j + 1, :] * inverse
        pivot_right = right[j : j + 1, :] * inverse
        wide = jnp.where(sublane == j, pivot, wide - column * pivot)
        right = jnp.where(sublane == j, pivot_right, right - column * pivot_right)
    out[0:vectors] = right
    out[vectors : 2 * vectors] = pltpu.roll(wide, states - vectors, 1)
    out[2 * vectors : 3 * vectors] = jnp.broadcast_to(diagonal, (vectors, states))


def grams(mine, near, far, both, table, own, gram, sigmas):
    targets, vectors, states = mine.shape
    first = lax.axis_index("tgt") * targets
    sigmas[...] = (mine[...] + near[...]) + (far[...] + both[...])
    own[...] = sigmas[lax.axis_index("src")]
    block = jnp.concatenate([table[first + i] for i in range(targets)], axis=1)
    wide = jnp.concatenate([sigmas[i] for i in range(targets)], axis=1)
    small = contract(wide, jnp.concatenate([block, wide], axis=0))
    gram[...] = jnp.concatenate(
        [small, jnp.zeros((vectors, states - 2 * vectors), jnp.float32)], axis=1
    )


def finish(*refs):
    pieces, (solved, own, sigma, residual, norms) = refs[:-5], refs[-5:]
    vectors, states = own.shape
    pieces = [piece[...] for piece in pieces]
    while len(pieces) > 1:
        pieces = [left + right for left, right in zip(pieces[::2], pieces[1::2])]
    gram = pieces[0]
    lane = lax.broadcasted_iota(jnp.int32, (vectors, states), 1)
    sublane = lax.broadcasted_iota(jnp.int32, (vectors, states), 0)
    left = own[...]
    sigma[0] = left
    mixing = jnp.zeros((vectors, states), jnp.float32)
    for j in range(vectors):
        column = gram[:, j : j + 1]
        left = left - column * solved[j : j + 1, :]
        mixing = mixing + column * solved[vectors + j : vectors + j + 1, :]
    residual[0] = left
    terms = jnp.where(lane == sublane + vectors, gram, 0.0) - jnp.where(
        lane < vectors, gram * mixing, 0.0
    )
    totals = jnp.maximum(jnp.sum(terms, axis=1, keepdims=True), 0.0)
    column = jnp.sqrt(totals / solved[2 * vectors : 3 * vectors, :])
    norms[...] = jnp.sum(jnp.where(lane == sublane, column, 0.0), axis=0)[:vectors]


def shards(trial_vectors, couplings, neighbours, live_slots, energies):
    vectors, _, states = trial_vectors.shape
    targets = couplings.shape[0]
    src_count, tgt_count = lax.axis_size("src"), lax.axis_size("tgt")
    params = pltpu.CompilerParams(vmem_limit_bytes=LIMIT)

    def call(body, outs, in_specs, flops, moved, scratch=()):
        return pl.pallas_call(
            body,
            out_shape=outs,
            in_specs=in_specs,
            out_specs=jax.tree.map(lambda _: VMEM, outs),
            scratch_shapes=scratch,
            compiler_params=params,
            cost_estimate=pl.CostEstimate(
                flops=flops, bytes_accessed=moved, transcendentals=0
            ),
        )

    def shape(*dims, dtype=jnp.float32):
        return jax.ShapeDtypeStruct(dims, dtype)

    size = couplings.size
    row = jnp.transpose(trial_vectors, (1, 0, 2))
    count, slots = src_count * tgt_count, couplings.shape[1]
    side_shape = (vectors + 2 * slots, states)
    anywhere = pl.BlockSpec(memory_space=pl.ANY)
    copies, side = pl.pallas_call(
        spread,
        out_shape=(shape(count, vectors, states), shape(*side_shape)),
        in_specs=[anywhere] * 4,
        out_specs=[anywhere] * 2,
        scratch_shapes=[
            pltpu.VMEM(row.shape, jnp.float32),
            pltpu.VMEM((slots, targets), jnp.int32),
            pltpu.VMEM((slots, targets), jnp.int32),
            pltpu.VMEM(energies.shape, jnp.float32),
            pltpu.VMEM((count, vectors, states), jnp.float32),
            pltpu.VMEM(side_shape, jnp.float32),
            pltpu.SemaphoreType.DMA((4,)),
        ],
    )(row, neighbours.T, live_slots.T, energies)
    other_side = pair(side, (1, 2))
    other = pair(couplings, (1, 2))
    half = shape(targets, slots, 2 * states, states, dtype=jnp.bfloat16)
    halve = call(prepare, half, [VMEM] * 2, 4 * size, 8 * size)
    halves, other_halves = halve(couplings, side), halve(other, other_side)
    table = lax.all_to_all(copies, ("tgt", "src"), 0, 0, tiled=True)
    partial = call(
        products, shape(targets, vectors, states), [VMEM] * 5, 4 * size * vectors, 8 * size
    )(table, halves, side, other_halves, other_side)
    solved = call(invert, shape(3 * vectors, states), [VMEM], 10**6, 4 * table.size)(table)

    steps = [(bit, bit) for bit in bits_of(src_count)[2:]]
    for step in steps[1:]:
        partial = partial + pair(partial, step)
    near, far = (2, 1), steps[0]
    both = (near[0] ^ far[0], near[1] ^ far[1])
    parts = [pair(partial, step) for step in (near, far, both)]
    parts = [parts[n] for n in (0, 1, 2)]
    own, gram = call(
        grams,
        (shape(vectors, states), shape(vectors, states)),
        [VMEM] * 5,
        10**6,
        12 * partial.size,
        [pltpu.VMEM((targets, vectors, states), jnp.float32)],
    )(partial, *parts, table)

    for bit in reversed(bits_of(tgt_count)[2:]):
        gram = gram + exchange(gram, "tgt", bit)
    pieces = [exchange(gram, "tgt", bit) for bit in reversed(range(1, min(tgt_count, 4)))]
    pieces = pieces + [gram]
    sigma, residual, norms = call(
        finish,
        (shape(1, vectors, states), shape(1, vectors, states), shape(vectors)),
        [VMEM] * (len(pieces) + 2),
        10**4,
        10**5,
    )(*pieces, solved, own)
    return (jnp.transpose(sigma, (1, 0, 2)), jnp.transpose(residual, (1, 0, 2)), norms)


def solution(mesh):
    return jax.shard_map(
        shards,
        mesh=mesh,
        in_specs=(
            P(None, ("tgt", "src"), None),
            P("tgt", "src", None, None),
            P("tgt", "src"),
            P("tgt", "src"),
            P(("tgt", "src"), None),
        ),
        out_specs=(P(None, ("tgt", "src"), None), P(None, ("tgt", "src"), None), P()),
        check_vma=False,
    )
```

```python
import jax
import jax.numpy as jnp
from jax import lax
from jax.experimental import pallas as pl
from jax.experimental.pallas import tpu as pltpu
from jax.sharding import PartitionSpec as P

VMEM = pl.BlockSpec(memory_space=pltpu.VMEM)
LIMIT = 24 * 2**20


def exchange(x, axis, bit):
    count = lax.axis_size(axis)
    return lax.ppermute(x, axis, [(i, i ^ bit) for i in range(count)])


def pair(x, bits):
    tgt_count, src_count = lax.axis_size("tgt"), lax.axis_size("src")
    partners = [
        (t * src_count + s, t * src_count + (s ^ bits[t % 2]))
        for t in range(tgt_count)
        for s in range(src_count)
    ]
    return lax.ppermute(x, ("tgt", "src"), partners)


def bits_of(count):
    return [1 << n for n in range(count.bit_length() - 1)]


def split(x):
    high = x.astype(jnp.bfloat16)
    return high, (x - high.astype(jnp.float32)).astype(jnp.bfloat16)


def spread(row, neighbours, live, energies, copies, side, own, at, alive, energy, filled, packed, sems):
    slots, targets = live.shape
    vectors = own.shape[1]
    inward = [
        pltpu.make_async_copy(source, target, sems.at[n])
        for n, (source, target) in enumerate(
            [(row, own), (neighbours, at), (live, alive), (energies, energy)]
        )
    ]
    for move in inward:
        move.start()
    inward[0].wait()
    for i in range(filled.shape[0]):
        filled[i] = own[0]
    outward = pltpu.make_async_copy(filled, copies, sems.at[0])
    outward.start()
    for move in inward[1:]:
        move.wait()
    packed[...] = jnp.zeros_like(packed)
    packed[0:vectors] = own[0] * energy[...]
    packed[vectors : vectors + slots, 0:targets] = at[...].astype(jnp.float32)
    packed[vectors + slots : vectors + 2 * slots, 0:targets] = alive[...].astype(jnp.float32)
    sent = pltpu.make_async_copy(packed, side, sems.at[1])
    sent.start()
    outward.wait()
    sent.wait()


def prepare(couplings, side, halves):
    targets, slots, states = couplings.shape[:3]
    first = side.shape[0] - slots
    for i in range(targets):
        for n in range(slots):
            weight = side[first + n : first + n + 1, i : i + 1]
            halves[i, n, :states], halves[i, n, states:] = split(couplings[i, n] * weight)


def times(left, right):
    return lax.dot_general(
        left, right, (((1,), (1,)), ((), ())), preferred_element_type=jnp.float32
    )


def products(table, halves, side, other_halves, other_side, partial):
    targets, slots = halves.shape[0], halves.shape[1]
    vectors, states = table.shape[1:]
    own_src = lax.axis_index("src")
    away = 1 + lax.axis_index("tgt") % 2
    at = side[vectors : vectors + slots].astype(jnp.int32)
    other_at = other_side[vectors : vectors + slots].astype(jnp.int32)
    for i in range(targets):
        total = None
        for n in range(slots):
            rows = jnp.concatenate([table[at[n, i]], table[other_at[n, i]]], axis=1)
            term = times(
                jnp.concatenate(split(rows), axis=0),
                jnp.concatenate([halves[i, n], other_halves[i, n]], axis=1),
            )
            total = term if total is None else total + term
        total = total[:, :states] + total[:, states:]
        partial[i] = total[:vectors] + total[vectors:]
    partial[own_src] = partial[own_src] + side[0:vectors]
    partial[own_src ^ away] = partial[own_src ^ away] + other_side[0:vectors]


def contract(left, right):
    return lax.dot_general(
        left,
        right,
        (((1,), (1,)), ((), ())),
        precision=lax.Precision.HIGHEST,
        preferred_element_type=jnp.float32,
    )


def invert(table, out):
    rows, vectors, states = table.shape
    metric = jnp.zeros((vectors, vectors), jnp.float32)
    step = 32
    for r in range(0, rows, step):
        part = jnp.concatenate([table[i] for i in range(r, min(r + step, rows))], axis=1)
        metric = metric + contract(part, part)
    eye = (
        lax.broadcasted_iota(jnp.int32, (vectors, vectors), 0)
        == lax.broadcasted_iota(jnp.int32, (vectors, vectors), 1)
    )
    diagonal = jnp.sum(jnp.where(eye, metric, 0.0), axis=1, keepdims=True)
    sublane = lax.broadcasted_iota(jnp.int32, (vectors, states), 0)
    right = table[lax.axis_index("tgt") * lax.axis_size("src") + lax.axis_index("src")]
    wide = jnp.concatenate(
        [metric, jnp.where(eye, 1.0, 0.0), jnp.zeros((vectors, states - 2 * vectors), jnp.float32)],
        axis=1,
    )
    for j in range(vectors):
        column = wide[:, j : j + 1]
        inverse = 1.0 / wide[j : j + 1, j : j + 1]
        pivot = wide[j : j + 1, :] * inverse
        pivot_right = right[j : j + 1, :] * inverse
        wide = jnp.where(sublane == j, pivot, wide - column * pivot)
        right = jnp.where(sublane == j, pivot_right, right - column * pivot_right)
    out[0:vectors] = right
    out[vectors : 2 * vectors] = pltpu.roll(wide, states - vectors, 1)
    out[2 * vectors : 3 * vectors] = jnp.broadcast_to(diagonal, (vectors, states))


def grams(mine, near, far, both, table, own, gram, sigmas):
    targets, vectors, states = mine.shape
    first = lax.axis_index("tgt") * targets
    sigmas[...] = (mine[...] + near[...]) + (far[...] + both[...])
    own[...] = sigmas[lax.axis_index("src")]
    block = jnp.concatenate([table[first + i] for i in range(targets)], axis=1)
    wide = jnp.concatenate([sigmas[i] for i in range(targets)], axis=1)
    small = contract(wide, jnp.concatenate([block, wide], axis=0))
    gram[...] = jnp.concatenate(
        [small, jnp.zeros((vectors, states - 2 * vectors), jnp.float32)], axis=1
    )


def finish(*refs):
    pieces, (solved, own, sigma, residual, norms) = refs[:-5], refs[-5:]
    vectors, states = own.shape
    pieces = [piece[...] for piece in pieces]
    while len(pieces) > 1:
        pieces = [left + right for left, right in zip(pieces[::2], pieces[1::2])]
    gram = pieces[0]
    lane = lax.broadcasted_iota(jnp.int32, (vectors, states), 1)
    sublane = lax.broadcasted_iota(jnp.int32, (vectors, states), 0)
    left = own[...]
    sigma[0] = left
    mixing = jnp.zeros((vectors, states), jnp.float32)
    for j in range(vectors):
        column = gram[:, j : j + 1]
        left = left - column * solved[j : j + 1, :]
        mixing = mixing + column * solved[vectors + j : vectors + j + 1, :]
    residual[0] = left
    terms = jnp.where(lane == sublane + vectors, gram, 0.0) - jnp.where(
        lane < vectors, gram * mixing, 0.0
    )
    totals = jnp.maximum(jnp.sum(terms, axis=1, keepdims=True), 0.0)
    column = jnp.sqrt(totals / solved[2 * vectors : 3 * vectors, :])
    norms[...] = jnp.sum(jnp.where(lane == sublane, column, 0.0), axis=0)[:vectors]


def shards(trial_vectors, couplings, neighbours, live_slots, energies):
    vectors, _, states = trial_vectors.shape
    targets = couplings.shape[0]
    src_count, tgt_count = lax.axis_size("src"), lax.axis_size("tgt")
    params = pltpu.CompilerParams(vmem_limit_bytes=LIMIT)

    def call(body, outs, in_specs, flops, moved, scratch=()):
        return pl.pallas_call(
            body,
            out_shape=outs,
            in_specs=in_specs,
            out_specs=jax.tree.map(lambda _: VMEM, outs),
            scratch_shapes=scratch,
            compiler_params=params,
            cost_estimate=pl.CostEstimate(
                flops=flops, bytes_accessed=moved, transcendentals=0
            ),
        )

    def shape(*dims, dtype=jnp.float32):
        return jax.ShapeDtypeStruct(dims, dtype)

    size = couplings.size
    row = jnp.transpose(trial_vectors, (1, 0, 2))
    count, slots = src_count * tgt_count, couplings.shape[1]
    side_shape = (vectors + 2 * slots, states)
    anywhere = pl.BlockSpec(memory_space=pl.ANY)
    copies, side = pl.pallas_call(
        spread,
        out_shape=(shape(count, vectors, states), shape(*side_shape)),
        in_specs=[anywhere] * 4,
        out_specs=[anywhere] * 2,
        scratch_shapes=[
            pltpu.VMEM(row.shape, jnp.float32),
            pltpu.VMEM((slots, targets), jnp.int32),
            pltpu.VMEM((slots, targets), jnp.int32),
            pltpu.VMEM(energies.shape, jnp.float32),
            pltpu.VMEM((count, vectors, states), jnp.float32),
            pltpu.VMEM(side_shape, jnp.float32),
            pltpu.SemaphoreType.DMA((4,)),
        ],
    )(row, neighbours.T, live_slots.T, energies)
    other_side = pair(side, (1, 2))
    other = pair(couplings, (1, 2))
    half = shape(targets, slots, 2 * states, states, dtype=jnp.bfloat16)
    halve = call(prepare, half, [VMEM] * 2, 4 * size, 8 * size)
    halves, other_halves = halve(couplings, side), halve(other, other_side)
    table = lax.all_to_all(copies, ("tgt", "src"), 0, 0, tiled=True)
    partial = call(
        products, shape(targets, vectors, states), [VMEM] * 5, 4 * size * vectors, 8 * size
    )(table, halves, side, other_halves, other_side)
    solved = call(invert, shape(3 * vectors, states), [VMEM], 10**6, 4 * table.size)(table)

    steps = [(bit, bit) for bit in bits_of(src_count)[2:]]
    for step in steps[1:]:
        partial = partial + pair(partial, step)
    near, far = (2, 1), steps[0]
    both = (near[0] ^ far[0], near[1] ^ far[1])
    parts = [pair(partial, step) for step in (near, far, both)]
    parts = [parts[n] for n in (0, 1, 2)]
    parts[0], solved = lax.optimization_barrier((parts[0], solved))
    own, gram = call(
        grams,
        (shape(vectors, states), shape(vectors, states)),
        [VMEM] * 5,
        10**6,
        12 * partial.size,
        [pltpu.VMEM((targets, vectors, states), jnp.float32)],
    )(partial, *parts, table)

    for bit in reversed(bits_of(tgt_count)[2:]):
        gram = gram + exchange(gram, "tgt", bit)
    pieces = [exchange(gram, "tgt", bit) for bit in reversed(range(1, min(tgt_count, 4)))]
    pieces = pieces + [gram]
    sigma, residual, norms = call(
        finish,
        (shape(1, vectors, states), shape(1, vectors, states), shape(vectors)),
        [VMEM] * (len(pieces) + 2),
        10**4,
        10**5,
    )(*pieces, solved, own)
    return (jnp.transpose(sigma, (1, 0, 2)), jnp.transpose(residual, (1, 0, 2)), norms)


def solution(mesh):
    return jax.shard_map(
        shards,
        mesh=mesh,
        in_specs=(
            P(None, ("tgt", "src"), None),
            P("tgt", "src", None, None),
            P("tgt", "src"),
            P("tgt", "src"),
            P(("tgt", "src"), None),
        ),
        out_specs=(P(None, ("tgt", "src"), None), P(None, ("tgt", "src"), None), P()),
        check_vma=False,
    )
```
